32 devices in a mesh: dom: 4 (over z), dp: 8 (over y, x, core).
Axes of the slice: x: 2, y: 2, z: 4, core: 2. Of those that a mesh axis runs over, the one named last changes fastest.
Arguments:
- state: bfloat16 [8, 4096, 512], P('dp', 'dom'), may hold values from -6 to 6
- blocks: bfloat16 [32, 4, 128, 128], P('dom'), may hold values from -0.25 to 0.25
- source: int32 [32, 4], P('dom'), may hold values from 0 to 11
- count: int32 [32], P('dom'), may hold values from 1 to 4, as said below
- cotangent: bfloat16 [8, 4096, 512], P('dp', 'dom'), may hold values from -6 to 6
- w_self: bfloat16 [3, 512, 512], replicated, may hold values from -0.25 to 0.25
- w_nbr: bfloat16 [3, 512, 512], replicated, may hold values from -0.25 to 0.25
Outputs:
- final_state: bfloat16 [8, 4096, 512], P('dp', 'dom')
- state_grad: bfloat16 [8, 4096, 512], P('dp', 'dom')
- self_grad: float32 [3, 512, 512], replicated
- nbr_grad: float32 [3, 512, 512], replicated
The draws below stay inside these ranges and needn't reach their ends.
Inputs may be any that keep to these rules, and one draw needn't show every extreme that they name: `source`: index into the partition's extended tiles: the last 2 tiles of the previous partition (cyclically), then its own 8 tiles, then the first 2 tiles of the next partition. Slots at or past the count are unused.
All inputs are finite; a program needn't handle non-finite values.
Results may differ from the reference program's by a relative error of at most 0.015.
Values may be sent and summed in bfloat16 or wider, within the bound.
A program may use at most 128 MiB of HBM per device.

```python
import jax
import jax.numpy as jnp
from jax import lax

F = 512
TB = 128
TILE_DEV = 8
HALO = 2
NBR = 4
LAYERS = 3
TILES_TOTAL = 32
NODES = 4096
SAMPLES = 8


def draw_count(key, part):
    key = jax.random.fold_in(key, 7)
    tile_ids = jnp.arange(TILES_TOTAL, dtype=jnp.int32)
    topmost = 1 + tile_ids * NBR // TILES_TOTAL
    random_bits = jax.random.randint(key, (TILES_TOTAL,), 0, 1 << 20, dtype=jnp.int32)
    counts = 1 + random_bits % topmost
    return jnp.where(tile_ids == TILES_TOTAL - 1, NBR, counts).astype(jnp.int32)


def touch_ends(values, own_key, smallest, high):
    index_at = [jax.random.randint(jax.random.fold_in(own_key, axis), (), 0, length) for axis, length in enumerate(values.shape)]
    longest = values.shape.index(max(values.shape))
    next_to = index_at[:longest] + [(index_at[longest] + 1) % values.shape[longest]] + index_at[longest + 1:]
    return values.at[tuple(index_at)].set(smallest).at[tuple(next_to)].set(high)


def steps_of(own_key, dims, pieces, smallest, high):
    loudness = 1.0
    for position, blocks in pieces:
        draws = jax.random.uniform(jax.random.fold_in(jax.random.fold_in(own_key, 6), position), (blocks,), jnp.float32, smallest / len(pieces), high / len(pieces))
        loudness = loudness * jnp.repeat(jnp.exp(draws), dims[position] // blocks).reshape((-1,) + (1,) * (len(dims) - 1 - position))
    return loudness


def centred(rng, shape, scale, reach, pieces=(), kind=jnp.bfloat16):
    result = jax.random.normal(rng, shape, jnp.float32) * scale
    if len(pieces) > 0:
        result = steps_of(rng, shape, pieces, -0.22, 0.18) * result
    return jnp.clip(result, min=-reach, max=reach).astype(kind)


def setup_inputs(seed: int = 0) -> dict:
    seeds = jax.random.split(jax.random.key(seed), 8)
    state = centred(seeds[0], (SAMPLES, NODES, F), 1.0, 6.0, ((0, 8), (1, 4)))
    blocks = centred(seeds[1], (TILES_TOTAL, NBR, TB, TB), (TB * NBR) ** -0.5, 0.25, ((0, 4),))
    source = touch_ends(jax.random.randint(seeds[2], (TILES_TOTAL, NBR), 0, TILE_DEV + 2 * HALO), jax.random.fold_in(seeds[2], 1), 0, (TILE_DEV + 2 * HALO) - 1).astype(jnp.int32)
    count = draw_count(jax.random.fold_in(seeds[7], 71), 0)
    cotangent = centred(seeds[4], (SAMPLES, NODES, F), 1.0, 6.0, ((0, 8), (1, 4)))
    w_self = centred(seeds[5], (LAYERS, F, F), F ** -0.5, 0.25)
    w_nbr = centred(seeds[6], (LAYERS, F, F), F ** -0.5, 0.25)
    return dict(state=state, blocks=blocks, source=source, count=count, cotangent=cotangent, w_self=w_self, w_nbr=w_nbr)


def masked_blocks(blocks, count):
    live_slots = (jnp.arange(NBR, dtype=jnp.int32)[None, :] < count[:, None]).astype(jnp.bfloat16)
    return blocks * live_slots[:, :, None, None]


def reference(state, blocks, source, count, cotangent, w_self, w_nbr):
    weights_f = masked_blocks(blocks, count).astype(jnp.float32)
    owner = (jnp.arange(TILES_TOTAL, dtype=jnp.int32) // TILE_DEV) * TILE_DEV
    global_src = ((owner[:, None] + source - HALO) % TILES_TOTAL).astype(jnp.int32)
    flat_src = global_src.reshape(-1)

    def per_sample(totals, sample_pair):
        sample, cot_sample = sample_pair
        hidden = sample
        inputs, aggregates, preacts = [], [], []
        for stratum in range(LAYERS):
            tiles = hidden.reshape(TILES_TOTAL, TB, F).astype(jnp.float32)
            aggregate = jnp.einsum("tsab,tsbf->taf", weights_f, tiles[global_src]).reshape(NODES, F).astype(jnp.bfloat16)
            preact = jnp.dot(hidden, w_self[stratum], preferred_element_type=jnp.float32) + jnp.dot(aggregate, w_nbr[stratum], preferred_element_type=jnp.float32)
            inputs.append(hidden)
            aggregates.append(aggregate)
            preacts.append(preact)
            hidden = (hidden.astype(jnp.float32) + jax.nn.silu(preact)).astype(jnp.bfloat16)
        grad_now = cot_sample.astype(jnp.float32)
        self_parts, nbr_parts = [], []
        for stratum in reversed(range(LAYERS)):
            preact = preacts[stratum]
            sigmoid_pre = jax.nn.sigmoid(preact)
            grad_pre = (grad_now * sigmoid_pre * (1.0 + preact * (1.0 - sigmoid_pre))).astype(jnp.bfloat16)
            self_parts.append(jnp.dot(inputs[stratum].T, grad_pre, preferred_element_type=jnp.float32))
            nbr_parts.append(jnp.dot(aggregates[stratum].T, grad_pre, preferred_element_type=jnp.float32))
            grad_agg = jnp.dot(grad_pre, w_nbr[stratum].T, preferred_element_type=jnp.float32).astype(jnp.bfloat16)
            contrib = jnp.einsum("tsba,taf->tsbf", weights_f, grad_agg.reshape(TILES_TOTAL, TB, F).astype(jnp.float32))
            back = jax.ops.segment_sum(contrib.reshape(TILES_TOTAL * NBR, TB, F), flat_src, num_segments=TILES_TOTAL).reshape(NODES, F)
            grad_now = grad_now + jnp.dot(grad_pre, w_self[stratum].T, preferred_element_type=jnp.float32) + back
        self_stack = jnp.stack(self_parts[::-1])
        nbr_stack = jnp.stack(nbr_parts[::-1])
        return (totals[0] + self_stack, totals[1] + nbr_stack), (hidden, grad_now.astype(jnp.bfloat16))

    zeros_init = jnp.zeros((LAYERS, F, F), jnp.float32)
    sums, outputs = lax.scan(per_sample, (zeros_init, zeros_init), (state, cotangent))
    factor = float(SAMPLES * NODES) ** -0.5
    return outputs[0], outputs[1], sums[0] * factor, sums[1] * factor
```

```python
import functools
import math

import jax
import jax.numpy as jnp
from jax import lax
from jax.experimental import pallas as pl
from jax.experimental.pallas import tpu as pltpu
from jax.sharding import PartitionSpec as P

HALO = 2
LAYERS = 3
MESH = pl.DeviceIdType.MESH
F32 = jnp.float32
BF16 = jnp.bfloat16


def dot(a, b):
    return jnp.dot(a, b, preferred_element_type=F32)


def dot_nt(a, b):
    return lax.dot_general(a, b, (((1,), (1,)), ((), ())), preferred_element_type=F32)


def flip(x):
    return x.astype(F32).T.astype(BF16)


def kernel(
    n, k, state, blocks, source, count, cot, w_self, w_nbr,
    final, sgrad, gout,
    ext, adj, adj_back, hid_t, agg_t, agg_b, slope, pre_s, agg_s, grad, gpre, gagg,
    bsend, brecv, buf, rbuf, zbuf,
    fh_send, fh_recv, bh_send, bh_recv, rs_send, rs_recv, zr_send, zr_recv,
    zg_send, zg_recv, ag_send, ag_recv,
):
    dom, dp = lax.axis_index("dom"), lax.axis_index("dp")
    tiles, slots, tb, _ = blocks.shape
    rows, feat = state.shape
    rim = HALO * tb
    ext_tiles = tiles + 2 * HALO
    chunks = rows // rim
    wide = 2 * feat
    own = pl.ds(rim, rows)
    nxt = lax.rem(dom + 1, n)
    prv = lax.rem(dom + n - 1, n)

    def chunk(c):
        return pl.ds(pl.multiple_of(c * rim, rim), rim)

    def ext_chunk(c):
        return pl.ds(pl.multiple_of((c + 1) * rim, rim), rim)

    def bit_of(b):
        return lax.rem(lax.div(dp, 1 << b), 2)

    def partner(b):
        return dp + (1 - 2 * bit_of(b)) * (1 << b)

    barrier = pltpu.get_barrier_semaphore()
    for j in range(1, n):
        pl.semaphore_signal(
            barrier, inc=1, device_id={"dom": lax.rem(dom + j, n)}, device_id_type=MESH
        )
    for b in range(k):
        pl.semaphore_signal(barrier, inc=1, device_id={"dp": partner(b)}, device_id_type=MESH)
    pl.semaphore_wait(barrier, n - 1 + k)

    def remote(src, dst, send, recv, where):
        copy = pltpu.make_async_remote_copy(
            src_ref=src, dst_ref=dst, send_sem=send, recv_sem=recv,
            device_id=where, device_id_type=MESH,
        )
        copy.start()
        return copy

    def send_low(l, src):
        return remote(
            src, ext.at[l, pl.ds(rim + rows, rim)], fh_send.at[l, 0], fh_recv.at[l, 0],
            {"dom": prv},
        )

    def send_high(l, src):
        return remote(
            src, ext.at[l, pl.ds(0, rim)], fh_send.at[l, 1], fh_recv.at[l, 1], {"dom": nxt}
        )

    halo = [
        send_low(0, state.at[pl.ds(0, rim)]),
        send_high(0, state.at[pl.ds(rows - rim, rim)]),
    ]

    def load_state(c, _):
        ext[0, ext_chunk(c)] = state[chunk(c)]
        return 0

    lax.fori_loop(0, chunks, load_state, 0)

    def build(t, _):
        live = count[t]
        t_rows = pl.ds(pl.multiple_of(t * tb, tb), tb)
        weights = [blocks[t, s].astype(F32) for s in range(slots)]
        for u in range(ext_tiles):
            tile = jnp.zeros((tb, tb), F32)
            for s in range(slots):
                use = jnp.where((source[t, s] == u) & (live > s), 1.0, 0.0).astype(F32)
                tile = tile + weights[s] * use
            adj[t_rows, pl.ds(u * tb, tb)] = tile.astype(BF16)
            adj_back[pl.ds(u * tb, tb), t_rows] = tile.astype(BF16)
        return 0

    lax.fori_loop(0, tiles, build, 0)

    def finish(l, c):
        r, e = chunk(c), ext_chunk(c)
        agg = (
            agg_s[r]
            + dot(adj[r, pl.ds(0, rim)], ext[l, pl.ds(0, rim)])
            + dot(adj[r, pl.ds(rim + rows, rim)], ext[l, pl.ds(rim + rows, rim)])
        ).astype(BF16)
        agg_b[r] = agg
        pre = pre_s[r] + dot(agg, w_nbr[l])
        sig = jax.nn.sigmoid(pre)
        slope[l, r] = sig * (1.0 + pre * (1.0 - sig))
        hidden = (ext[l, e].astype(F32) + pre * sig).astype(BF16)
        if l < LAYERS - 1:
            ext[l + 1, e] = hidden
        else:
            final[r] = hidden

    def flip_agg(l):
        def body(c, _):
            agg_t[l, :, chunk(c)] = flip(agg_b[chunk(c)])
            return 0

        lax.fori_loop(0, chunks, body, 0)

    for l in range(LAYERS):
        if l > 0:
            flip_agg(l - 1)

        def before(c, _):
            r, e = chunk(c), ext_chunk(c)
            mine = ext[l, e]
            pre_s[r] = dot(mine, w_self[l])
            agg_s[r] = dot(adj[r, own], ext[l, own])
            hid_t[l, :, r] = flip(mine)
            return 0

        lax.fori_loop(0, chunks, before, 0)
        for copy in halo:
            copy.wait()
        halo = []
        finish(l, 0)
        if l < LAYERS - 1:
            halo.append(send_low(l + 1, ext.at[l + 1, pl.ds(rim, rim)]))
        finish(l, chunks - 1)
        if l < LAYERS - 1:
            halo.append(send_high(l + 1, ext.at[l + 1, pl.ds(rows, rim)]))

        def middle(c, _):
            finish(l, c)
            return 0

        lax.fori_loop(1, chunks - 1, middle, 0)

    half_cols = feat // 2
    rest = list(range(1, k))
    orders = ([0] + rest, [0] + rest[::-1])

    def summed(l):
        offs = [[0], [0]]
        lens = [wide >> s for s in range(k + 1)]
        for s in range(k + 1):
            flights = []
            if s < k:
                size = lens[s + 1]
                for q in range(2):
                    bit, off = bit_of(orders[q][s]), offs[q][s]
                    give = pl.multiple_of(off + (1 - bit) * size, size)
                    cols = pl.ds(q * half_cols, half_cols)
                    flights.append(
                        remote(
                            buf.at[l, pl.ds(give, size), cols],
                            rbuf.at[l, pl.ds(wide - lens[s], size), cols],
                            rs_send.at[l, q, s], rs_recv.at[l, q, s],
                            {"dp": partner(orders[q][s])},
                        )
                    )
                    offs[q].append(pl.multiple_of(off + bit * size, size))
                yield
                for copy in flights:
                    copy.wait()
                for q in range(2):
                    cols = pl.ds(q * half_cols, half_cols)
                    keep = pl.ds(offs[q][s + 1], size)
                    got = rbuf[l, pl.ds(wide - lens[s], size), cols].astype(F32)
                    buf[l, keep, cols] = (buf[l, keep, cols].astype(F32) + got).astype(BF16)
        piece_rows = zbuf.shape[3]
        across = half_cols // zbuf.shape[4]

        def piece(q, j):
            row = offs[q][k] + lax.div(j, across) * piece_rows
            col = q * half_cols + lax.rem(j, across) * zbuf.shape[4]
            return (
                pl.ds(pl.multiple_of(row, piece_rows), piece_rows),
                pl.ds(pl.multiple_of(col, zbuf.shape[4]), zbuf.shape[4]),
            )

        flights = []
        for j in range(1, n):
            peer = lax.rem(dom + j, n)
            for q in range(2):
                pr, pc = piece(q, peer)
                flights.append(
                    remote(
                        buf.at[l, pr, pc], zbuf.at[l, q, j],
                        zr_send.at[l, q, j], zr_recv.at[l, q, j], {"dom": peer},
                    )
                )
        yield
        for copy in flights:
            copy.wait()
        flights = []
        for q in range(2):
            pr, pc = piece(q, dom)
            total = buf[l, pr, pc].astype(F32)
            for j in range(1, n):
                total = total + zbuf[l, q, j].astype(F32)
            gout[l, pr, pc] = total.astype(BF16)
            for j in range(1, n):
                flights.append(
                    remote(
                        gout.at[l, pr, pc], gout.at[l, pr, pc],
                        zg_send.at[l, q, j], zg_recv.at[l, q, j],
                        {"dom": lax.rem(dom + j, n)},
                    )
                )
        yield
        for copy in flights:
            copy.wait()
        for s in reversed(range(k)):
            flights = []
            for q in range(2):
                where = (
                    l, pl.ds(offs[q][s + 1], lens[s + 1]), pl.ds(q * half_cols, half_cols)
                )
                flights.append(
                    remote(
                        gout.at[where], gout.at[where],
                        ag_send.at[l, q, s], ag_recv.at[l, q, s],
                        {"dp": partner(orders[q][s])},
                    )
                )
            yield
            for copy in flights:
                copy.wait()

    def advance(steps, times):
        for _ in range(times):
            next(steps, None)

    def load_cot(c, _):
        grad[chunk(c)] = cot[chunk(c)].astype(F32)
        return 0

    lax.fori_loop(0, chunks, load_cot, 0)

    def push(l, c):
        r = chunk(c)
        g = (grad[r] * slope[l, r]).astype(BF16)
        gpre[r] = g
        gagg[r] = dot_nt(g, w_nbr[l]).astype(BF16)

    def receive(l, flights):
        for copy in flights:
            copy.wait()
        first, last = pl.ds(0, rim), pl.ds(rows - rim, rim)
        grad[first] = grad[first] + brecv[l, 0].astype(F32)
        grad[last] = grad[last] + brecv[l, 1].astype(F32)

    halo, older = [], iter(())
    for l in reversed(range(LAYERS)):

        def inner(c, _):
            push(l, c)
            return 0

        lax.fori_loop(1, chunks - 1, inner, 0)
        if l < LAYERS - 1:
            receive(l + 1, halo)
        push(l, 0)
        push(l, chunks - 1)
        bsend[l, 0] = dot(adj_back[pl.ds(0, rim)], gagg[...]).astype(BF16)
        halo = [
            remote(
                bsend.at[l, 0], brecv.at[l, 1], bh_send.at[l, 0], bh_recv.at[l, 0],
                {"dom": prv},
            )
        ]
        bsend[l, 1] = dot(adj_back[pl.ds(rim + rows, rim)], gagg[...]).astype(BF16)
        halo.append(
            remote(
                bsend.at[l, 1], brecv.at[l, 0], bh_send.at[l, 1], bh_recv.at[l, 1],
                {"dom": nxt},
            )
        )
        advance(older, 1)
        if l == LAYERS - 1:
            flip_agg(l)

        def weights(c, _):
            r = chunk(c)
            buf[l, r] = dot(hid_t[l, r], gpre[...]).astype(BF16)
            buf[l, pl.ds(pl.multiple_of(feat + c * rim, rim), rim)] = dot(
                agg_t[l, r], gpre[...]
            ).astype(BF16)
            return 0

        lax.fori_loop(0, feat // rim, weights, 0)
        newer = summed(l)
        advance(newer, 1)
        advance(older, 1)

        def onward(c, _):
            r = chunk(c)
            grad[r] = grad[r] + dot_nt(gpre[r], w_self[l]) + dot(adj_back[ext_chunk(c)], gagg[...])
            return 0

        lax.fori_loop(0, chunks, onward, 0)
        for _ in range(k):
            advance(newer, 1)
            advance(older, 1)
        for _ in older:
            pass
        older = newer
    receive(0, halo)

    def store(c, _):
        sgrad[chunk(c)] = grad[chunk(c)].astype(BF16)
        return 0

    lax.fori_loop(0, chunks, store, 0)
    for _ in older:
        pass


def per_device(n, d, state, blocks, source, count, cotangent, w_self, w_nbr):
    tiles, slots, tb, _ = blocks.shape
    samples, rows, feat = state.shape
    rim = HALO * tb
    extent = rows + 2 * rim
    wide = 2 * feat
    k = d.bit_length() - 1
    across = feat // 2 // 128
    piece_rows = (wide >> k) // (n // across)
    vmem = pl.BlockSpec(memory_space=pltpu.VMEM)
    smem = pl.BlockSpec(memory_space=pltpu.SMEM)
    dma = pltpu.SemaphoreType.DMA
    scratch = [
        pltpu.VMEM((LAYERS, extent, feat), BF16),
        pltpu.VMEM((rows, extent), BF16),
        pltpu.VMEM((extent, rows), BF16),
        pltpu.VMEM((LAYERS, feat, rows), BF16),
        pltpu.VMEM((LAYERS, feat, rows), BF16),
        pltpu.VMEM((rows, feat), BF16),
        pltpu.VMEM((LAYERS, rows, feat), F32),
        pltpu.VMEM((rows, feat), F32),
        pltpu.VMEM((rows, feat), F32),
        pltpu.VMEM((rows, feat), F32),
        pltpu.VMEM((rows, feat), BF16),
        pltpu.VMEM((rows, feat), BF16),
        pltpu.VMEM((LAYERS, 2, rim, feat), BF16),
        pltpu.VMEM((LAYERS, 2, rim, feat), BF16),
        pltpu.VMEM((LAYERS, wide, feat), BF16),
        pltpu.VMEM((LAYERS, wide, feat), BF16),
        pltpu.VMEM((LAYERS, 2, n, piece_rows, 128), BF16),
        dma((LAYERS, 2)), dma((LAYERS, 2)), dma((LAYERS, 2)), dma((LAYERS, 2)),
        dma((LAYERS, 2, k)), dma((LAYERS, 2, k)),
        dma((LAYERS, 2, n)), dma((LAYERS, 2, n)),
        dma((LAYERS, 2, n)), dma((LAYERS, 2, n)),
        dma((LAYERS, 2, k)), dma((LAYERS, 2, k)),
    ]
    final, sgrad, gout = pl.pallas_call(
        functools.partial(kernel, n, k),
        out_shape=(
            jax.ShapeDtypeStruct((rows, feat), BF16),
            jax.ShapeDtypeStruct((rows, feat), BF16),
            jax.ShapeDtypeStruct((LAYERS, wide, feat), BF16),
        ),
        in_specs=[vmem, vmem, smem, smem, vmem, vmem, vmem],
        out_specs=(vmem, vmem, vmem),
        scratch_shapes=scratch,
        compiler_params=pltpu.CompilerParams(
            collective_id=0, has_side_effects=True, vmem_limit_bytes=60 * 1024 * 1024
        ),
    )(
        state.reshape(samples * rows, feat), blocks, source, count,
        cotangent.reshape(samples * rows, feat), w_self, w_nbr,
    )
    factor = 1.0 / math.sqrt(rows * samples * n * d)
    grads = gout.astype(F32) * factor
    return final[None], sgrad[None], grads[:, :feat], grads[:, feat:]


def solution(mesh):
    in_specs = (
        P("dp", "dom", None),
        P("dom", None, None, None),
        P("dom", None),
        P("dom"),
        P("dp", "dom", None),
        P(),
        P(),
    )
    out_specs = (P("dp", "dom", None), P("dp", "dom", None), P(), P())
    return jax.shard_map(
        functools.partial(per_device, mesh.shape["dom"], mesh.shape["dp"]),
        mesh=mesh, in_specs=in_specs, out_specs=out_specs, check_vma=False,
    )
```

```python
import functools
import math

import jax
import jax.numpy as jnp
from jax import lax
from jax.experimental import pallas as pl
from jax.experimental.pallas import tpu as pltpu
from jax.sharding import PartitionSpec as P

HALO = 2
LAYERS = 3
MESH = pl.DeviceIdType.MESH
F32 = jnp.float32
BF16 = jnp.bfloat16


def dot(a, b):
    return jnp.dot(a, b, preferred_element_type=F32)


def dot_nt(a, b):
    return lax.dot_general(a, b, (((1,), (1,)), ((), ())), preferred_element_type=F32)


def flip(x):
    return x.astype(F32).T.astype(BF16)


def kernel(
    n, k, state, blocks, source, count, cot, w_self, w_nbr,
    final, sgrad, gout,
    ext, adj, adj_back, hid_t, agg_t, agg_b, slope, pre_s, agg_s, grad, gpre, gagg,
    bsend, brecv, buf, rbuf, zbuf,
    fh_send, fh_recv, bh_send, bh_recv, rs_send, rs_recv, zr_send, zr_recv,
    zg_send, zg_recv, ag_send, ag_recv,
):
    dom, dp = lax.axis_index("dom"), lax.axis_index("dp")
    tiles, slots, tb, _ = blocks.shape
    rows, feat = state.shape
    rim = HALO * tb
    ext_tiles = tiles + 2 * HALO
    chunks = rows // rim
    wide = 2 * feat
    own = pl.ds(rim, rows)
    nxt = lax.rem(dom + 1, n)
    prv = lax.rem(dom + n - 1, n)

    def chunk(c):
        return pl.ds(pl.multiple_of(c * rim, rim), rim)

    def ext_chunk(c):
        return pl.ds(pl.multiple_of((c + 1) * rim, rim), rim)

    def bit_of(b):
        return lax.rem(lax.div(dp, 1 << b), 2)

    def partner(b):
        return dp + (1 - 2 * bit_of(b)) * (1 << b)

    barrier = pltpu.get_barrier_semaphore()
    for j in range(1, n):
        pl.semaphore_signal(
            barrier, inc=1, device_id={"dom": lax.rem(dom + j, n)}, device_id_type=MESH
        )
    for b in range(k):
        pl.semaphore_signal(barrier, inc=1, device_id={"dp": partner(b)}, device_id_type=MESH)
    pl.semaphore_wait(barrier, n - 1 + k)

    def remote(src, dst, send, recv, where):
        copy = pltpu.make_async_remote_copy(
            src_ref=src, dst_ref=dst, send_sem=send, recv_sem=recv,
            device_id=where, device_id_type=MESH,
        )
        copy.start()
        return copy

    def send_low(l, src):
        return remote(
            src, ext.at[l, pl.ds(rim + rows, rim)], fh_send.at[l, 0], fh_recv.at[l, 0],
            {"dom": prv},
        )

    def send_high(l, src):
        return remote(
            src, ext.at[l, pl.ds(0, rim)], fh_send.at[l, 1], fh_recv.at[l, 1], {"dom": nxt}
        )

    halo = [
        send_low(0, state.at[pl.ds(0, rim)]),
        send_high(0, state.at[pl.ds(rows - rim, rim)]),
    ]

    def load_state(c, _):
        ext[0, ext_chunk(c)] = state[chunk(c)]
        return 0

    lax.fori_loop(0, chunks, load_state, 0)

    def build(t, _):
        live = count[t]
        t_rows = pl.ds(pl.multiple_of(t * tb, tb), tb)
        weights = [blocks[t, s].astype(F32) for s in range(slots)]
        for u in range(ext_tiles):
            tile = jnp.zeros((tb, tb), F32)
            for s in range(slots):
                use = jnp.where((source[t, s] == u) & (live > s), 1.0, 0.0).astype(F32)
                tile = tile + weights[s] * use
            adj[t_rows, pl.ds(u * tb, tb)] = tile.astype(BF16)
            adj_back[pl.ds(u * tb, tb), t_rows] = tile.astype(BF16)
        return 0

    lax.fori_loop(0, tiles, build, 0)

    def finish(l, c):
        r, e = chunk(c), ext_chunk(c)
        agg = (
            agg_s[r]
            + dot(adj[r, pl.ds(0, rim)], ext[l, pl.ds(0, rim)])
            + dot(adj[r, pl.ds(rim + rows, rim)], ext[l, pl.ds(rim + rows, rim)])
        ).astype(BF16)
        agg_b[r] = agg
        pre = pre_s[r] + dot(agg, w_nbr[l])
        sig = jax.nn.sigmoid(pre)
        slope[l, r] = sig * (1.0 + pre * (1.0 - sig))
        hidden = (ext[l, e].astype(F32) + pre * sig).astype(BF16)
        if l < LAYERS - 1:
            ext[l + 1, e] = hidden
        else:
            final[r] = hidden

    def flip_agg(l):
        def body(c, _):
            agg_t[l, :, chunk(c)] = flip(agg_b[chunk(c)])
            return 0

        lax.fori_loop(0, chunks, body, 0)

    for l in range(LAYERS):
        if l > 0:
            flip_agg(l - 1)

        def before(c, _):
            r, e = chunk(c), ext_chunk(c)
            mine = ext[l, e]
            pre_s[r] = dot(mine, w_self[l])
            agg_s[r] = dot(adj[r, own], ext[l, own])
            hid_t[l, :, r] = flip(mine)
            return 0

        lax.fori_loop(0, chunks, before, 0)
        for copy in halo:
            copy.wait()
        halo = []
        finish(l, 0)
        if l < LAYERS - 1:
            halo.append(send_low(l + 1, ext.at[l + 1, pl.ds(rim, rim)]))
        finish(l, chunks - 1)
        if l < LAYERS - 1:
            halo.append(send_high(l + 1, ext.at[l + 1, pl.ds(rows, rim)]))

        def middle(c, _):
            finish(l, c)
            return 0

        lax.fori_loop(1, chunks - 1, middle, 0)

    half_cols = feat // 2
    rest = list(range(1, k))
    orders = ([0] + rest, [0] + rest[::-1])

    def summed(l):
        offs = [[0], [0]]
        lens = [wide >> s for s in range(k + 1)]
        for s in range(k + 1):
            flights = []
            if s < k:
                size = lens[s + 1]
                for q in range(2):
                    bit, off = bit_of(orders[q][s]), offs[q][s]
                    give = pl.multiple_of(off + (1 - bit) * size, size)
                    cols = pl.ds(q * half_cols, half_cols)
                    flights.append(
                        remote(
                            buf.at[l, pl.ds(give, size), cols],
                            rbuf.at[l, pl.ds(wide - lens[s], size), cols],
                            rs_send.at[l, q, s], rs_recv.at[l, q, s],
                            {"dp": partner(orders[q][s])},
                        )
                    )
                    offs[q].append(pl.multiple_of(off + bit * size, size))
                yield
                for copy in flights:
                    copy.wait()
                for q in range(2):
                    cols = pl.ds(q * half_cols, half_cols)
                    keep = pl.ds(offs[q][s + 1], size)
                    got = rbuf[l, pl.ds(wide - lens[s], size), cols].astype(F32)
                    buf[l, keep, cols] = (buf[l, keep, cols].astype(F32) + got).astype(BF16)
        piece_rows = zbuf.shape[3]
        across = half_cols // zbuf.shape[4]

        def piece(q, j):
            row = offs[q][k] + lax.div(j, across) * piece_rows
            col = q * half_cols + lax.rem(j, across) * zbuf.shape[4]
            return (
                pl.ds(pl.multiple_of(row, piece_rows), piece_rows),
                pl.ds(pl.multiple_of(col, zbuf.shape[4]), zbuf.shape[4]),
            )

        flights = []
        for j in range(1, n):
            peer = lax.rem(dom + j, n)
            for q in range(2):
                pr, pc = piece(q, peer)
                flights.append(
                    remote(
                        buf.at[l, pr, pc], zbuf.at[l, q, j],
                        zr_send.at[l, q, j], zr_recv.at[l, q, j], {"dom": peer},
                    )
                )
        yield
        for copy in flights:
            copy.wait()
        flights = []
        for q in range(2):
            pr, pc = piece(q, dom)
            total = buf[l, pr, pc].astype(F32)
            for j in range(1, n):
                total = total + zbuf[l, q, j].astype(F32)
            gout[l, pr, pc] = total.astype(BF16)
            for j in range(1, n):
                flights.append(
                    remote(
                        gout.at[l, pr, pc], gout.at[l, pr, pc],
                        zg_send.at[l, q, j], zg_recv.at[l, q, j],
                        {"dom": lax.rem(dom + j, n)},
                    )
                )
        yield
        for copy in flights:
            copy.wait()
        for s in reversed(range(k)):
            flights = []
            for q in range(2):
                where = (
                    l, pl.ds(offs[q][s + 1], lens[s + 1]), pl.ds(q * half_cols, half_cols)
                )
                flights.append(
                    remote(
                        gout.at[where], gout.at[where],
                        ag_send.at[l, q, s], ag_recv.at[l, q, s],
                        {"dp": partner(orders[q][s])},
                    )
                )
            yield
            for copy in flights:
                copy.wait()

    def advance(steps, times):
        for _ in range(times):
            next(steps, None)

    def load_cot(c, _):
        grad[chunk(c)] = cot[chunk(c)].astype(F32)
        return 0

    lax.fori_loop(0, chunks, load_cot, 0)

    def push(l, c):
        r = chunk(c)
        g = (grad[r] * slope[l, r]).astype(BF16)
        gpre[r] = g
        gagg[r] = dot_nt(g, w_nbr[l]).astype(BF16)

    def receive(l, flights):
        for copy in flights:
            copy.wait()
        first, last = pl.ds(0, rim), pl.ds(rows - rim, rim)
        grad[first] = grad[first] + brecv[l, 0].astype(F32)
        grad[last] = grad[last] + brecv[l, 1].astype(F32)

    def weigh(l):
        def weights(c, _):
            r = chunk(c)
            buf[l, r] = dot(hid_t[l, r], gpre[...]).astype(BF16)
            buf[l, pl.ds(pl.multiple_of(feat + c * rim, rim), rim)] = dot(
                agg_t[l, r], gpre[...]
            ).astype(BF16)
            return 0

        lax.fori_loop(0, feat // rim, weights, 0)
        steps = summed(l)
        advance(steps, 1)
        return steps

    halo, older, oldest = [], iter(()), iter(())
    for l in reversed(range(LAYERS)):

        def inner(c, _):
            push(l, c)
            return 0

        lax.fori_loop(1, chunks - 1, inner, 0)
        if l < LAYERS - 1:
            receive(l + 1, halo)
        push(l, 0)
        push(l, chunks - 1)
        if l == 0:
            newer = weigh(l)
        bsend[l, 0] = dot(adj_back[pl.ds(0, rim)], gagg[...]).astype(BF16)
        halo = [
            remote(
                bsend.at[l, 0], brecv.at[l, 1], bh_send.at[l, 0], bh_recv.at[l, 0],
                {"dom": prv},
            )
        ]
        bsend[l, 1] = dot(adj_back[pl.ds(rim + rows, rim)], gagg[...]).astype(BF16)
        halo.append(
            remote(
                bsend.at[l, 1], brecv.at[l, 0], bh_send.at[l, 1], bh_recv.at[l, 1],
                {"dom": nxt},
            )
        )
        advance(older, 1)
        advance(oldest, 1)
        if l == LAYERS - 1:
            flip_agg(l)
        if l == 0:
            advance(newer, 1)
        else:
            newer = weigh(l)
        advance(oldest, 1)

        def onward(c, _):
            r = chunk(c)
            grad[r] = grad[r] + dot_nt(gpre[r], w_self[l]) + dot(adj_back[ext_chunk(c)], gagg[...])
            return 0

        lax.fori_loop(0, chunks, onward, 0)
        for _ in range(k if l > 0 else k - 1):
            advance(newer, 1)
            advance(oldest, 1)
        for _ in oldest:
            pass
        if l > 0:
            oldest, older = older, newer
    advance(older, 1)
    advance(newer, 1)
    receive(0, halo)

    def store(c, _):
        sgrad[chunk(c)] = grad[chunk(c)].astype(BF16)
        return 0

    lax.fori_loop(0, chunks, store, 0)
    for _ in range(k + 1):
        advance(older, 1)
        advance(newer, 1)


def per_device(n, d, state, blocks, source, count, cotangent, w_self, w_nbr):
    tiles, slots, tb, _ = blocks.shape
    samples, rows, feat = state.shape
    rim = HALO * tb
    extent = rows + 2 * rim
    wide = 2 * feat
    k = d.bit_length() - 1
    across = feat // 2 // 128
    piece_rows = (wide >> k) // (n // across)
    vmem = pl.BlockSpec(memory_space=pltpu.VMEM)
    smem = pl.BlockSpec(memory_space=pltpu.SMEM)
    dma = pltpu.SemaphoreType.DMA
    scratch = [
        pltpu.VMEM((LAYERS, extent, feat), BF16),
        pltpu.VMEM((rows, extent), BF16),
        pltpu.VMEM((extent, rows), BF16),
        pltpu.VMEM((LAYERS, feat, rows), BF16),
        pltpu.VMEM((LAYERS, feat, rows), BF16),
        pltpu.VMEM((rows, feat), BF16),
        pltpu.VMEM((LAYERS, rows, feat), F32),
        pltpu.VMEM((rows, feat), F32),
        pltpu.VMEM((rows, feat), F32),
        pltpu.VMEM((rows, feat), F32),
        pltpu.VMEM((rows, feat), BF16),
        pltpu.VMEM((rows, feat), BF16),
        pltpu.VMEM((LAYERS, 2, rim, feat), BF16),
        pltpu.VMEM((LAYERS, 2, rim, feat), BF16),
        pltpu.VMEM((LAYERS, wide, feat), BF16),
        pltpu.VMEM((LAYERS, wide, feat), BF16),
        pltpu.VMEM((LAYERS, 2, n, piece_rows, 128), BF16),
        dma((LAYERS, 2)), dma((LAYERS, 2)), dma((LAYERS, 2)), dma((LAYERS, 2)),
        dma((LAYERS, 2, k)), dma((LAYERS, 2, k)),
        dma((LAYERS, 2, n)), dma((LAYERS, 2, n)),
        dma((LAYERS, 2, n)), dma((LAYERS, 2, n)),
        dma((LAYERS, 2, k)), dma((LAYERS, 2, k)),
    ]
    final, sgrad, gout = pl.pallas_call(
        functools.partial(kernel, n, k),
        out_shape=(
            jax.ShapeDtypeStruct((rows, feat), BF16),
            jax.ShapeDtypeStruct((rows, feat), BF16),
            jax.ShapeDtypeStruct((LAYERS, wide, feat), BF16),
        ),
        in_specs=[vmem, vmem, smem, smem, vmem, vmem, vmem],
        out_specs=(vmem, vmem, vmem),
        scratch_shapes=scratch,
        compiler_params=pltpu.CompilerParams(
            collective_id=0, has_side_effects=True, vmem_limit_bytes=60 * 1024 * 1024
        ),
    )(
        state.reshape(samples * rows, feat), blocks, source, count,
        cotangent.reshape(samples * rows, feat), w_self, w_nbr,
    )
    factor = 1.0 / math.sqrt(rows * samples * n * d)
    return (
        final[None],
        sgrad[None],
        gout[:, :feat].astype(F32) * factor,
        gout[:, feat:].astype(F32) * factor,
    )


def solution(mesh):
    in_specs = (
        P("dp", "dom", None),
        P("dom", None, None, None),
        P("dom", None),
        P("dom"),
        P("dp", "dom", None),
        P(),
        P(),
    )
    out_specs = (P("dp", "dom", None), P("dp", "dom", None), P(), P())
    return jax.shard_map(
        functools.partial(per_device, mesh.shape["dom"], mesh.shape["dp"]),
        mesh=mesh, in_specs=in_specs, out_specs=out_specs, check_vma=False,
    )
```

```python
import functools
import math

import jax
import jax.numpy as jnp
from jax import lax
from jax.experimental import pallas as pl
from jax.experimental.pallas import tpu as pltpu
from jax.sharding import PartitionSpec as P

HALO = 2
LAYERS = 3
MESH = pl.DeviceIdType.MESH
F32 = jnp.float32
BF16 = jnp.bfloat16


def dot(a, b):
    return jnp.dot(a, b, preferred_element_type=F32)


def dot_nt(a, b):
    return lax.dot_general(a, b, (((1,), (1,)), ((), ())), preferred_element_type=F32)


def flip(x):
    return x.astype(F32).T.astype(BF16)


def kernel(
    n, k, state, blocks, source, count, cot_in, w_self_in, w_nbr_in,
    final, sgrad, gout,
    ext, adj, adj_back, hid_t, agg_t, agg_b, slope, pre_s, agg_s, grad, gpre, gagg,
    bsend, brecv, buf, rbuf, zbuf, cot, w_self, w_nbr, load_sem,
    fh_send, fh_recv, bh_send, bh_recv, rs_send, rs_recv, zr_send, zr_recv,
    zg_send, zg_recv, ag_send, ag_recv,
):
    dom, dp = lax.axis_index("dom"), lax.axis_index("dp")
    tiles, slots, tb, _ = blocks.shape
    rows, feat = state.shape
    rim = HALO * tb
    ext_tiles = tiles + 2 * HALO
    chunks = rows // rim
    wide = 2 * feat
    own = pl.ds(rim, rows)
    nxt = lax.rem(dom + 1, n)
    prv = lax.rem(dom + n - 1, n)

    def chunk(c):
        return pl.ds(pl.multiple_of(c * rim, rim), rim)

    def ext_chunk(c):
        return pl.ds(pl.multiple_of((c + 1) * rim, rim), rim)

    def bit_of(b):
        return lax.rem(lax.div(dp, 1 << b), 2)

    def partner(b):
        return dp + (1 - 2 * bit_of(b)) * (1 << b)

    loads = [
        pltpu.make_async_copy(w_self_in, w_self, load_sem.at[0]),
        pltpu.make_async_copy(w_nbr_in, w_nbr, load_sem.at[1]),
        pltpu.make_async_copy(cot_in, cot, load_sem.at[2]),
    ]
    for load in loads:
        load.start()

    barrier = pltpu.get_barrier_semaphore()
    for j in range(1, n):
        pl.semaphore_signal(
            barrier, inc=1, device_id={"dom": lax.rem(dom + j, n)}, device_id_type=MESH
        )
    for b in range(k):
        pl.semaphore_signal(barrier, inc=1, device_id={"dp": partner(b)}, device_id_type=MESH)
    pl.semaphore_wait(barrier, n - 1 + k)

    def remote(src, dst, send, recv, where):
        copy = pltpu.make_async_remote_copy(
            src_ref=src, dst_ref=dst, send_sem=send, recv_sem=recv,
            device_id=where, device_id_type=MESH,
        )
        copy.start()
        return copy

    def send_low(l, src):
        return remote(
            src, ext.at[l, pl.ds(rim + rows, rim)], fh_send.at[l, 0], fh_recv.at[l, 0],
            {"dom": prv},
        )

    def send_high(l, src):
        return remote(
            src, ext.at[l, pl.ds(0, rim)], fh_send.at[l, 1], fh_recv.at[l, 1], {"dom": nxt}
        )

    halo = [
        send_low(0, state.at[pl.ds(0, rim)]),
        send_high(0, state.at[pl.ds(rows - rim, rim)]),
    ]

    def load_state(c, _):
        ext[0, ext_chunk(c)] = state[chunk(c)]
        return 0

    lax.fori_loop(0, chunks, load_state, 0)

    def build(t, _):
        live = count[t]
        t_rows = pl.ds(pl.multiple_of(t * tb, tb), tb)
        weights = [blocks[t, s].astype(F32) for s in range(slots)]
        for u in range(ext_tiles):
            tile = jnp.zeros((tb, tb), F32)
            for s in range(slots):
                use = jnp.where((source[t, s] == u) & (live > s), 1.0, 0.0).astype(F32)
                tile = tile + weights[s] * use
            adj[t_rows, pl.ds(u * tb, tb)] = tile.astype(BF16)
            adj_back[pl.ds(u * tb, tb), t_rows] = tile.astype(BF16)
        return 0

    lax.fori_loop(0, tiles, build, 0)
    for load in loads:
        load.wait()

    def finish(l, c):
        r, e = chunk(c), ext_chunk(c)
        agg = (
            agg_s[r]
            + dot(adj[r, pl.ds(0, rim)], ext[l, pl.ds(0, rim)])
            + dot(adj[r, pl.ds(rim + rows, rim)], ext[l, pl.ds(rim + rows, rim)])
        ).astype(BF16)
        agg_b[r] = agg
        pre = pre_s[r] + dot(agg, w_nbr[l])
        sig = jax.nn.sigmoid(pre)
        slope[l, r] = sig * (1.0 + pre * (1.0 - sig))
        hidden = (ext[l, e].astype(F32) + pre * sig).astype(BF16)
        if l < LAYERS - 1:
            ext[l + 1, e] = hidden
        else:
            final[r] = hidden

    def flip_agg(l):
        def body(c, _):
            agg_t[l, :, chunk(c)] = flip(agg_b[chunk(c)])
            return 0

        lax.fori_loop(0, chunks, body, 0)

    for l in range(LAYERS):
        if l > 0:
            flip_agg(l - 1)

        def before(c, _):
            r, e = chunk(c), ext_chunk(c)
            mine = ext[l, e]
            pre_s[r] = dot(mine, w_self[l])
            agg_s[r] = dot(adj[r, own], ext[l, own])
            hid_t[l, :, r] = flip(mine)
            return 0

        lax.fori_loop(0, chunks, before, 0)
        for copy in halo:
            copy.wait()
        halo = []
        finish(l, 0)
        if l < LAYERS - 1:
            halo.append(send_low(l + 1, ext.at[l + 1, pl.ds(rim, rim)]))
        finish(l, chunks - 1)
        if l < LAYERS - 1:
            halo.append(send_high(l + 1, ext.at[l + 1, pl.ds(rows, rim)]))

        def middle(c, _):
            finish(l, c)
            return 0

        lax.fori_loop(1, chunks - 1, middle, 0)

    half_cols = feat // 2
    rest = list(range(1, k))
    orders = ([0] + rest, [0] + rest[::-1])

    def summed(l):
        offs = [[0], [0]]
        lens = [wide >> s for s in range(k + 1)]
        for s in range(k + 1):
            flights = []
            if s < k:
                size = lens[s + 1]
                for q in range(2):
                    bit, off = bit_of(orders[q][s]), offs[q][s]
                    give = pl.multiple_of(off + (1 - bit) * size, size)
                    cols = pl.ds(q * half_cols, half_cols)
                    flights.append(
                        remote(
                            buf.at[l, pl.ds(give, size), cols],
                            rbuf.at[l, pl.ds(wide - lens[s], size), cols],
                            rs_send.at[l, q, s], rs_recv.at[l, q, s],
                            {"dp": partner(orders[q][s])},
                        )
                    )
                    offs[q].append(pl.multiple_of(off + bit * size, size))
                yield
                for copy in flights:
                    copy.wait()
                for q in range(2):
                    cols = pl.ds(q * half_cols, half_cols)
                    keep = pl.ds(offs[q][s + 1], size)
                    got = rbuf[l, pl.ds(wide - lens[s], size), cols].astype(F32)
                    buf[l, keep, cols] = (buf[l, keep, cols].astype(F32) + got).astype(BF16)
        piece_rows = zbuf.shape[3]
        across = half_cols // zbuf.shape[4]

        def piece(q, j):
            row = offs[q][k] + lax.div(j, across) * piece_rows
            col = q * half_cols + lax.rem(j, across) * zbuf.shape[4]
            return (
                pl.ds(pl.multiple_of(row, piece_rows), piece_rows),
                pl.ds(pl.multiple_of(col, zbuf.shape[4]), zbuf.shape[4]),
            )

        flights = []
        for j in range(1, n):
            peer = lax.rem(dom + j, n)
            for q in range(2):
                pr, pc = piece(q, peer)
                flights.append(
                    remote(
                        buf.at[l, pr, pc], zbuf.at[l, q, j],
                        zr_send.at[l, q, j], zr_recv.at[l, q, j], {"dom": peer},
                    )
                )
        yield
        for copy in flights:
            copy.wait()
        flights = []
        for q in range(2):
            pr, pc = piece(q, dom)
            total = buf[l, pr, pc].astype(F32)
            for j in range(1, n):
                total = total + zbuf[l, q, j].astype(F32)
            gout[l, pr, pc] = total.astype(BF16)
            for j in range(1, n):
                flights.append(
                    remote(
                        gout.at[l, pr, pc], gout.at[l, pr, pc],
                        zg_send.at[l, q, j], zg_recv.at[l, q, j],
                        {"dom": lax.rem(dom + j, n)},
                    )
                )
        yield
        for copy in flights:
            copy.wait()
        for s in reversed(range(k)):
            flights = []
            for q in range(2):
                where = (
                    l, pl.ds(offs[q][s + 1], lens[s + 1]), pl.ds(q * half_cols, half_cols)
                )
                flights.append(
                    remote(
                        gout.at[where], gout.at[where],
                        ag_send.at[l, q, s], ag_recv.at[l, q, s],
                        {"dp": partner(orders[q][s])},
                    )
                )
            yield
            for copy in flights:
                copy.wait()

    def advance(steps, times):
        for _ in range(times):
            next(steps, None)

    def load_cot(c, _):
        grad[chunk(c)] = cot[chunk(c)].astype(F32)
        return 0

    lax.fori_loop(0, chunks, load_cot, 0)

    def push(l, c):
        r = chunk(c)
        g = (grad[r] * slope[l, r]).astype(BF16)
        gpre[r] = g
        gagg[r] = dot_nt(g, w_nbr[l]).astype(BF16)

    def receive(l, flights):
        for copy in flights:
            copy.wait()
        first, last = pl.ds(0, rim), pl.ds(rows - rim, rim)
        grad[first] = grad[first] + brecv[l, 0].astype(F32)
        grad[last] = grad[last] + brecv[l, 1].astype(F32)

    mid = pl.ds(rim, rows - 2 * rim)
    ends = (pl.ds(0, rim), pl.ds(rows - rim, rim))
    rims = (pl.ds(0, rim), pl.ds(rim + rows, rim))

    def weigh_mid(l):
        def weights(c, _):
            r = chunk(c)
            pre_s[r] = dot(hid_t[l, r, mid], gpre[mid])
            pre_s[pl.ds(pl.multiple_of(feat + c * rim, rim), rim)] = dot(
                agg_t[l, r, mid], gpre[mid]
            )
            return 0

        lax.fori_loop(0, feat // rim, weights, 0)

    def weigh(l):
        def weights(c, _):
            r = chunk(c)
            low = pl.ds(pl.multiple_of(feat + c * rim, rim), rim)
            top, bottom = pre_s[r], pre_s[low]
            for end in ends:
                top = top + dot(hid_t[l, r, end], gpre[end])
                bottom = bottom + dot(agg_t[l, r, end], gpre[end])
            buf[l, r] = top.astype(BF16)
            buf[l, low] = bottom.astype(BF16)
            return 0

        lax.fori_loop(0, feat // rim, weights, 0)
        steps = summed(l)
        advance(steps, 1)
        return steps

    def back_mid():
        for i in range(2):
            agg_s[pl.ds(i * rim, rim)] = dot(adj_back[rims[i], mid], gagg[mid])

    def back(i):
        total = agg_s[pl.ds(i * rim, rim)]
        for end in ends:
            total = total + dot(adj_back[rims[i], end], gagg[end])
        return total.astype(BF16)

    halo, older, oldest = [], iter(()), iter(())
    for l in reversed(range(LAYERS)):

        def inner(c, _):
            push(l, c)
            return 0

        lax.fori_loop(1, chunks - 1, inner, 0)
        back_mid()
        if l < LAYERS - 1:
            weigh_mid(l)
            receive(l + 1, halo)
        push(l, 0)
        push(l, chunks - 1)
        if l == 0:
            newer = weigh(l)
        bsend[l, 0] = back(0)
        halo = [
            remote(
                bsend.at[l, 0], brecv.at[l, 1], bh_send.at[l, 0], bh_recv.at[l, 0],
                {"dom": prv},
            )
        ]
        bsend[l, 1] = back(1)
        halo.append(
            remote(
                bsend.at[l, 1], brecv.at[l, 0], bh_send.at[l, 1], bh_recv.at[l, 1],
                {"dom": nxt},
            )
        )
        if l == 0:
            advance(newer, 1)
        advance(older, 1)
        advance(oldest, 1)
        if l == LAYERS - 1:
            flip_agg(l)
            weigh_mid(l)
        if l > 0:
            newer = weigh(l)
        advance(oldest, 1)

        def onward(c, _):
            r = chunk(c)
            grad[r] = grad[r] + dot_nt(gpre[r], w_self[l]) + dot(adj_back[ext_chunk(c)], gagg[...])
            return 0

        lax.fori_loop(0, chunks, onward, 0)
        for _ in range(k if l > 0 else k - 1):
            advance(newer, 1)
            advance(oldest, 1)
        for _ in oldest:
            pass
        if l > 0:
            oldest, older = older, newer
    advance(older, 1)
    advance(newer, 1)
    receive(0, halo)

    def store(c, _):
        sgrad[chunk(c)] = grad[chunk(c)].astype(BF16)
        return 0

    lax.fori_loop(0, chunks, store, 0)
    for _ in range(k + 1):
        advance(older, 1)
        advance(newer, 1)


def per_device(n, d, state, blocks, source, count, cotangent, w_self, w_nbr):
    tiles, slots, tb, _ = blocks.shape
    samples, rows, feat = state.shape
    rim = HALO * tb
    extent = rows + 2 * rim
    wide = 2 * feat
    k = d.bit_length() - 1
    across = feat // 2 // 128
    piece_rows = (wide >> k) // (n // across)
    vmem = pl.BlockSpec(memory_space=pltpu.VMEM)
    hbm = pl.BlockSpec(memory_space=pl.ANY)
    smem = pl.BlockSpec(memory_space=pltpu.SMEM)
    dma = pltpu.SemaphoreType.DMA
    scratch = [
        pltpu.VMEM((LAYERS, extent, feat), BF16),
        pltpu.VMEM((rows, extent), BF16),
        pltpu.VMEM((extent, rows), BF16),
        pltpu.VMEM((LAYERS, feat, rows), BF16),
        pltpu.VMEM((LAYERS, feat, rows), BF16),
        pltpu.VMEM((rows, feat), BF16),
        pltpu.VMEM((LAYERS, rows, feat), F32),
        pltpu.VMEM((rows, feat), F32),
        pltpu.VMEM((rows, feat), F32),
        pltpu.VMEM((rows, feat), F32),
        pltpu.VMEM((rows, feat), BF16),
        pltpu.VMEM((rows, feat), BF16),
        pltpu.VMEM((LAYERS, 2, rim, feat), BF16),
        pltpu.VMEM((LAYERS, 2, rim, feat), BF16),
        pltpu.VMEM((LAYERS, wide, feat), BF16),
        pltpu.VMEM((LAYERS, wide, feat), BF16),
        pltpu.VMEM((LAYERS, 2, n, piece_rows, 128), BF16),
        pltpu.VMEM((rows, feat), BF16),
        pltpu.VMEM(w_self.shape, BF16),
        pltpu.VMEM(w_nbr.shape, BF16),
        dma((3,)),
        dma((LAYERS, 2)), dma((LAYERS, 2)), dma((LAYERS, 2)), dma((LAYERS, 2)),
        dma((LAYERS, 2, k)), dma((LAYERS, 2, k)),
        dma((LAYERS, 2, n)), dma((LAYERS, 2, n)),
        dma((LAYERS, 2, n)), dma((LAYERS, 2, n)),
        dma((LAYERS, 2, k)), dma((LAYERS, 2, k)),
    ]
    final, sgrad, gout = pl.pallas_call(
        functools.partial(kernel, n, k),
        out_shape=(
            jax.ShapeDtypeStruct((rows, feat), BF16),
            jax.ShapeDtypeStruct((rows, feat), BF16),
            jax.ShapeDtypeStruct((LAYERS, wide, feat), BF16),
        ),
        in_specs=[vmem, vmem, smem, smem, hbm, hbm, hbm],
        out_specs=(vmem, vmem, vmem),
        scratch_shapes=scratch,
        compiler_params=pltpu.CompilerParams(
            collective_id=0, has_side_effects=True, vmem_limit_bytes=60 * 1024 * 1024
        ),
    )(
        state.reshape(samples * rows, feat), blocks, source, count,
        cotangent.reshape(samples * rows, feat), w_self, w_nbr,
    )
    factor = 1.0 / math.sqrt(rows * samples * n * d)
    return (
        final[None],
        sgrad[None],
        gout[:, :feat].astype(F32) * factor,
        gout[:, feat:].astype(F32) * factor,
    )


def solution(mesh):
    in_specs = (
        P("dp", "dom", None),
        P("dom", None, None, None),
        P("dom", None),
        P("dom"),
        P("dp", "dom", None),
        P(),
        P(),
    )
    out_specs = (P("dp", "dom", None), P("dp", "dom", None), P(), P())
    return jax.shard_map(
        functools.partial(per_device, mesh.shape["dom"], mesh.shape["dp"]),
        mesh=mesh, in_specs=in_specs, out_specs=out_specs, check_vma=False,
    )
```
